128 devices in a mesh: tm: 64 (over z, y, x), seq: 2 (over core).
Axes of the slice: x: 4, y: 4, z: 4, core: 2. Of those that a mesh axis runs over, the one named last changes fastest.
Arguments:
- starts: float32 [64, 64, 1024], P('tm', None, 'seq'), may hold values from -6 to 6
- w_embed: bfloat16 [64, 2432], replicated, may hold values from -0.75 to 0.75
- pos_embed: bfloat16 [1024, 2432], replicated, may hold values from -5 to 5
- mod_table: float32 [64, 3, 2432], replicated, may hold values from -5 to 5
- mod_index: int32 [64, 2], P('tm'), may hold values from 0 to 63
- w_qkv: bfloat16 [2432, 3, 1536], P(None, None, 'seq'), may hold values from -0.15625 to 0.15625
- w_out: bfloat16 [1536, 2432], P('seq'), may hold values from -0.15625 to 0.15625
- text_kv: bfloat16 [2, 333, 1536], P(None, None, 'seq'), may hold values from -160 to 160
- w_final: bfloat16 [2432, 64], replicated, may hold values from -0.3125 to 0.3125
Outputs:
- corrected: float32 [64, 64, 1024], P('tm', None, 'seq')
- first_velocity: float32 [64, 64, 1024], P('tm', None, 'seq')
The draws below stay inside these ranges and needn't reach their ends.
All inputs are finite; a program needn't handle non-finite values.
Results may differ from the reference program's by a relative error of at most 0.02.
The reference program's roundings to bfloat16 on the way count: a program that leaves them out, or rounds other values in their place, can miss the bound.
Values may be sent and summed in bfloat16 or wider, within the bound.
A program may use at most 192 MiB of HBM per device.

```python
import jax
import jax.numpy as jnp
from jax import lax

D = 2432
HD = 64
C = 64
H = 24
IMG = 1024
TXT = 333
LEVELS = 64
FINE = 2
HA = 1536
BLOCKS = 64


def draw_text_kv(key, part):
    key = jax.random.fold_in(key, 11)
    base_key = jax.random.fold_in(key, 0)
    return jnp.clip(jax.random.normal(base_key, (2, TXT, HA), jnp.float32), -6.0, 6.0).astype(jnp.bfloat16)


def touch_ends(array, rng, smallest, top_value):
    place = [jax.random.randint(jax.random.fold_in(rng, axis), (), 0, length) for axis, length in enumerate(array.shape)]
    main_axis = array.shape.index(max(array.shape))
    neighbour = place[:main_axis] + [(place[main_axis] + 1) % array.shape[main_axis]] + place[main_axis + 1:]
    return array.at[tuple(place)].set(smallest).at[tuple(neighbour)].set(top_value)


def block_scale(key, dims, pieces, smallest, high):
    factor_of = 1.0
    for position, parts in pieces:
        heights = jax.random.uniform(jax.random.fold_in(jax.random.fold_in(key, 6), position), (parts,), jnp.float32, smallest / len(pieces), high / len(pieces))
        factor_of = factor_of * jnp.repeat(jnp.exp(heights), dims[position] // parts).reshape((-1,) + (1,) * (len(dims) - 1 - position))
    return factor_of


def normal_values(key, shape, deviation, limit, pieces=(), dtype=jnp.bfloat16):
    array = jax.random.normal(key, shape, jnp.float32) * deviation
    if len(pieces) > 0:
        array = block_scale(key, shape, pieces, -0.22, 0.18) * array
    return jnp.clip(array, min=-limit, max=limit).astype(dtype)


def setup_inputs(seed: int = 0) -> dict:
    splits = jax.random.split(jax.random.key(seed), 10)
    return {
        "starts": normal_values(splits[0], (BLOCKS, C, IMG), 1.0, 6.0, ((0, 64), (2, 2)), jnp.float32),
        "w_embed": normal_values(splits[1], (C, D), C ** -0.5, 0.75),
        "pos_embed": normal_values(splits[2], (IMG, D), 1.0, 5.0),
        "mod_table": normal_values(splits[3], (LEVELS, 3, D), 1.0, 5.0, (), jnp.float32),
        "mod_index": touch_ends(jax.random.randint(splits[4], (BLOCKS, FINE), 0, LEVELS), jax.random.fold_in(splits[4], 1), 0, LEVELS - 1).astype(jnp.int32),
        "w_qkv": normal_values(splits[5], (D, 3, HA), (D // 2) ** -0.5, 0.15625, ((2, 2),)),
        "w_out": normal_values(splits[6], (HA, D), HA ** -0.5, 0.15625, ((0, 2),)),
        "text_kv": draw_text_kv(jax.random.fold_in(splits[9], 71), 0),
        "w_final": normal_values(splits[8], (D, C), (D // 8) ** -0.5, 0.3125),
    }


def layer_norm(values):
    row_mean = lax.optimization_barrier(jnp.mean(values, -1, keepdims=True))
    centered = values - row_mean
    variance = lax.optimization_barrier(jnp.mean(centered * centered, -1, keepdims=True))
    return centered * lax.rsqrt(variance + 1e-06)

def velocity(latent_state, mod_rows, w_embed, pos_embed, w_qkv, w_out, text_kv, w_final):
    latent = latent_state.astype(jnp.bfloat16)
    embedded = lax.dot_general(latent, w_embed, (((0,), (0,)), ((), ())), preferred_element_type=jnp.float32) + pos_embed.astype(jnp.float32)
    modulated = (layer_norm(embedded) * (1.0 + mod_rows[1]) + mod_rows[0]).astype(jnp.bfloat16)
    projected = jnp.dot(modulated, w_qkv.reshape(D, 3 * HA), preferred_element_type=jnp.float32).astype(jnp.bfloat16)
    queries = projected[:, :HA].reshape(IMG, H, HD)
    key_rows = jnp.concatenate([projected[:, HA:2 * HA], text_kv[0]], 0).reshape(IMG + TXT, H, HD).astype(jnp.float32)
    value_rows = jnp.concatenate([projected[:, 2 * HA:], text_kv[1]], 0).reshape(IMG + TXT, H, HD).astype(jnp.float32)
    query_block = min(512, IMG)
    grouped = queries.reshape(IMG // query_block, query_block, H, HD)

    def attend(query_part):
        scores = jnp.einsum('qhd,khd->hqk', query_part.astype(jnp.float32), key_rows) * HD ** (-0.5)
        probs = jax.nn.softmax(scores, axis=-1).astype(jnp.bfloat16)
        result = jnp.einsum('hqk,khd->qhd', probs.astype(jnp.float32), value_rows)
        return result.astype(jnp.bfloat16).reshape(query_block, HA)
    attended = lax.map(attend, grouped).reshape(IMG, HA)
    hidden = embedded + mod_rows[2] * jnp.dot(attended, w_out, preferred_element_type=jnp.float32)
    normed = layer_norm(hidden).astype(jnp.bfloat16)
    return lax.dot_general(w_final, normed, (((0,), (1,)), ((), ())), preferred_element_type=jnp.float32)

def reference(starts, w_embed, pos_embed, mod_table, mod_index, w_qkv, w_out, text_kv, w_final):
    step_total = BLOCKS * FINE
    grid_index = jnp.arange(step_total + 1).astype(jnp.float32)
    shifted = 1.0 - 0.95 * grid_index / step_total
    times = 3.0 * shifted / (1.0 + 2.0 * shifted)

    def solve_block(block_index):
        mod_rows = mod_table[mod_index[block_index]]
        latent_state = starts[block_index]
        first_velocity = None
        for substep in range(FINE):
            speed = velocity(latent_state, mod_rows[substep], w_embed, pos_embed, w_qkv, w_out, text_kv, w_final)
            if substep == 0:
                first_velocity = speed
            step_index = block_index * FINE + substep
            latent_state = latent_state + (times[step_index + 1] - times[step_index]) * speed
        return (latent_state, first_velocity)
    fine_ends, firsts = lax.map(solve_block, jnp.arange(BLOCKS).astype(jnp.int32))
    ratios = times[FINE::FINE] / times[0:step_total:FINE]

    def advance(new_start, inputs):
        decay_ratio, fine_end, block_start = inputs
        corrected_block = decay_ratio * new_start + (fine_end - decay_ratio * block_start)
        return (corrected_block, corrected_block)
    last_state, corrected = lax.scan(advance, starts[0], (ratios, fine_ends, starts))
    return (corrected, firsts)
```

```python
import functools
import math

import jax
import jax.numpy as jnp
from jax import lax
from jax.experimental import pallas as pl
from jax.experimental.pallas import tpu as pltpu
from jax.sharding import PartitionSpec as P

HD = 64
MESH = pl.DeviceIdType.MESH
F32 = jnp.float32
BF16 = jnp.bfloat16
TN = (((0,), (0,)), ((), ()))
NT = (((1,), (1,)), ((), ()))
RING = 4


def moment(step_index, step_total):
    shifted = 1.0 - 0.95 * step_index.astype(F32) / step_total
    return 3.0 * shifted / (1.0 + 2.0 * shifted)


def normalized(values):
    centered = values - jnp.mean(values, -1, keepdims=True)
    variance = jnp.mean(centered * centered, -1, keepdims=True)
    return centered * lax.rsqrt(variance + 1e-06)


def span(index, size, align):
    return pl.ds(pl.multiple_of(index * size, align), size)


def kernel(
    key_total,
    starts,
    w_embed,
    pos_hbm,
    mod_table,
    mod_index,
    w_qkv_hbm,
    w_out_hbm,
    text,
    w_final,
    corrected,
    first_velocity,
    pos,
    w_qkv,
    w_out,
    latents,
    state,
    modulated,
    queries,
    keys,
    values,
    scores_a,
    scores_b,
    attended,
    sums_out,
    sums_in,
    load_sem,
    latent_send,
    latent_recv,
    att_send,
    att_recv,
    wide_send,
    wide_recv,
    scan_send,
    scan_recv,
):
    own_block = lax.axis_index("tm")
    own = lax.axis_index("seq")
    blocks = lax.axis_size("tm")
    peer = {"tm": own_block, "seq": 1 - own}
    share = starts.shape[1]
    image = 2 * share
    head_cols = w_out_hbm.shape[0]
    heads = head_cols // HD
    fine_steps = mod_index.shape[1]
    step_total = blocks * fine_steps
    own_tokens = span(own, share, share)

    ring_axes = []
    for stride in (1, RING, RING * RING):
        place = (own_block // stride) % RING
        peers = []
        for distance in range(1, RING):
            target = own_block + ((place + distance) % RING - place) * stride
            peers.append({"tm": target, "seq": own})
        ring_axes.append((place, peers))

    barrier = pltpu.get_barrier_semaphore()
    greeted = [peer] + [device for _, peers in ring_axes for device in peers]
    for device in greeted:
        pl.semaphore_signal(barrier, inc=1, device_id=device, device_id_type=MESH)

    loads = [pltpu.make_async_copy(pos_hbm, pos, load_sem.at[0])]
    for part in range(3):
        loads.append(
            pltpu.make_async_copy(
                w_qkv_hbm.at[part], w_qkv.at[part], load_sem.at[1 + part]
            )
        )
    loads.append(pltpu.make_async_copy(w_out_hbm, w_out.at[0], load_sem.at[4]))
    for load in loads:
        load.start()

    state[...] = starts[...]
    latents[0, :, own_tokens] = starts[...].astype(BF16)
    pl.semaphore_wait(barrier, len(greeted))

    def latent_copy(step):
        return pltpu.make_async_remote_copy(
            src_ref=latents.at[step, :, own_tokens],
            dst_ref=latents.at[step, :, own_tokens],
            send_sem=latent_send.at[step],
            recv_sem=latent_recv.at[step],
            device_id=peer,
            device_id_type=MESH,
        )

    def attended_copy(step):
        return pltpu.make_async_remote_copy(
            src_ref=attended.at[0],
            dst_ref=attended.at[2],
            send_sem=att_send.at[step],
            recv_sem=att_recv.at[step],
            device_id=peer,
            device_id_type=MESH,
        )

    latent_copy(0).start()
    wide_copy = pltpu.make_async_remote_copy(
        src_ref=w_out_hbm,
        dst_ref=w_out.at[1],
        send_sem=wide_send,
        recv_sem=wide_recv,
        device_id=peer,
        device_id_type=MESH,
    )
    wide_copy.start()

    text_rows = text.shape[0]
    keys[image : image + text_rows, :] = text[:, :head_cols]
    values[:, image : image + text_rows] = text[:, head_cols:].T

    lane = lax.broadcasted_iota(jnp.int32, (1, 2 * HD), 1)
    key_row = lax.broadcasted_iota(jnp.int32, (8, 1), 0)
    key_rows = keys.shape[0]

    def score(index, buffer):
        index = jnp.minimum(index, 2 * heads - 1)
        tile = jnp.where(index < heads, 1 - own, own)
        head = index % heads
        pair = span(head // 2, 2 * HD, 2 * HD)
        query = queries[span(tile, share, share), pair]
        query = jnp.where(lane // HD == head % 2, query, jnp.zeros_like(query))
        buffer[...] = lax.dot_general(keys[:, pair], query, NT, preferred_element_type=F32)
        buffer[key_rows - 8 :, :] = jnp.where(
            key_row < key_total - (key_rows - 8), buffer[key_rows - 8 :, :], -1e30
        )

    def attend(index, buffer):
        head = index % heads
        rows = span(head, HD, HD)
        value = buffer[...]
        expanded = jnp.exp2(value - jnp.max(value, axis=0, keepdims=True))
        total = jnp.sum(expanded, axis=0, keepdims=True)
        result = jnp.dot(values[rows, :], expanded.astype(BF16), preferred_element_type=F32)
        attended[index // heads, rows, :] = (result / total).astype(BF16)

    def fine_step(step, carry):
        level = mod_index[0, step]
        shift = mod_table[0, pl.ds(level, 1), :]
        scale = 1.0 + mod_table[1, pl.ds(level, 1), :]
        gate = mod_table[2, pl.ds(level, 1), :]

        @pl.when(step == 0)
        def _():
            loads[0].wait()

        chunk = 256
        chunks = image // chunk

        def embed(tokens):
            embedded = lax.dot_general(
                latents[step, :, tokens], w_embed[...], TN, preferred_element_type=F32
            )
            return embedded + pos[tokens, :].astype(F32)

        def modulate(index, carry):
            @pl.when(index == chunks // 2)
            def _():
                latent_copy(step).wait_recv()

            tokens = span((own * (chunks // 2) + index) % chunks, chunk, chunk)
            modulated[tokens, :] = (normalized(embed(tokens)) * scale + shift).astype(BF16)
            return carry

        lax.fori_loop(0, chunks, modulate, 0)
        latent_copy(step).wait_send()

        @pl.when(step == 0)
        def _():
            for load in loads[1:4]:
                load.wait()

        def project(part):
            return jnp.dot(modulated[...], w_qkv[part], preferred_element_type=F32)

        queries[...] = (project(0) * (HD**-0.5 / math.log(2))).astype(BF16)
        keys[:image, :] = project(1).astype(BF16)
        values[:, :image] = project(2).astype(BF16).T

        score(0, scores_a)

        def pair_of_heads(index, carry):
            score(2 * index + 1, scores_b)
            attend(2 * index, scores_a)
            score(2 * index + 2, scores_a)
            attend(2 * index + 1, scores_b)
            return carry

        lax.fori_loop(0, heads // 2, pair_of_heads, 0)
        attended_copy(step).start()
        lax.fori_loop(heads // 2, heads, pair_of_heads, 0)
        attended_copy(step).wait()

        @pl.when(step == 0)
        def _():
            loads[4].wait()
            wide_copy.wait()

        fine_index = own_block * fine_steps + step
        pace = moment(fine_index + 1, step_total) - moment(fine_index, step_total)

        def finish(index, carry):
            within = span(index, chunk, chunk)
            tokens = span(own * (share // chunk) + index, chunk, chunk)
            mixed = lax.dot_general(
                attended[1, :, within], w_out[0], TN, preferred_element_type=F32
            ) + lax.dot_general(attended[2, :, within], w_out[1], TN, preferred_element_type=F32)
            hidden = embed(tokens) + gate * mixed
            normed = normalized(hidden).astype(BF16)
            speed = lax.dot_general(w_final[...], normed, NT, preferred_element_type=F32)
            state[:, within] = state[:, within] + pace * speed

            @pl.when(step == 0)
            def _():
                first_velocity[:, within] = speed

            return carry

        lax.fori_loop(0, share // chunk, finish, 0)

        @pl.when(step < fine_steps - 1)
        def _():
            latents[step + 1, :, own_tokens] = state[...].astype(BF16)
            latent_copy(step + 1).start()

        return carry

    lax.fori_loop(0, fine_steps, fine_step, 0)

    time_before = moment(own_block * fine_steps, step_total)
    time_after = moment((own_block + 1) * fine_steps, step_total)
    keep_start = jnp.where(own_block == 0, 0.0, 1.0)
    share_sum = state[...] / time_after - (keep_start / time_before) * starts[...]
    result = share_sum
    for axis, (place, peers) in enumerate(ring_axes):
        sums_out[axis] = share_sum.astype(BF16)
        copies = []
        for slot, device in enumerate(peers):
            copy = pltpu.make_async_remote_copy(
                src_ref=sums_out.at[axis],
                dst_ref=sums_in.at[axis, slot],
                send_sem=scan_send.at[axis, slot],
                recv_sem=scan_recv.at[axis, slot],
                device_id=device,
                device_id_type=MESH,
            )
            copy.start()
            copies.append(copy)
        for slot, copy in enumerate(copies):
            copy.wait()
            arrived = sums_in[axis, slot].astype(F32)
            earlier = jnp.where(place >= slot + 1, 1.0, 0.0)
            result = result + earlier * arrived
            share_sum = share_sum + arrived
    corrected[...] = time_after * result


def on_device(starts, w_embed, pos_embed, mod_table, mod_index, w_qkv, w_out, text_kv, w_final):
    channels, share = starts.shape[1:]
    image, width = pos_embed.shape
    head_cols = w_out.shape[0]
    text_total = text_kv.shape[1]
    text_rows = -(-text_total // 16) * 16
    key_rows = image + text_rows
    text = text_kv.transpose(1, 0, 2).reshape(text_total, 2 * head_cols)
    text = jnp.pad(text, ((0, text_rows - text_total), (0, 0)))
    vmem = pl.BlockSpec(memory_space=pltpu.VMEM)
    anywhere = pl.BlockSpec(memory_space=pl.ANY)
    corrected, first_velocity = pl.pallas_call(
        functools.partial(kernel, image + text_total),
        out_shape=[jax.ShapeDtypeStruct((channels, share), F32)] * 2,
        in_specs=[
            vmem,
            vmem,
            anywhere,
            vmem,
            pl.BlockSpec(memory_space=pltpu.SMEM),
            anywhere,
            anywhere,
            vmem,
            vmem,
        ],
        out_specs=[vmem, vmem],
        scratch_shapes=[
            pltpu.VMEM((image, width), BF16),
            pltpu.VMEM((3, width, head_cols), BF16),
            pltpu.VMEM((2, head_cols, width), BF16),
            pltpu.VMEM((2, channels, image), BF16),
            pltpu.VMEM((channels, share), F32),
            pltpu.VMEM((image, width), BF16),
            pltpu.VMEM((image, head_cols), BF16),
            pltpu.VMEM((key_rows, head_cols), BF16),
            pltpu.VMEM((head_cols, key_rows), BF16),
            pltpu.VMEM((key_rows, share), F32),
            pltpu.VMEM((key_rows, share), F32),
            pltpu.VMEM((3, head_cols, share), BF16),
            pltpu.VMEM((3, channels, share), BF16),
            pltpu.VMEM((3, RING - 1, channels, share), BF16),
            pltpu.SemaphoreType.DMA((5,)),
            pltpu.SemaphoreType.DMA((2,)),
            pltpu.SemaphoreType.DMA((2,)),
            pltpu.SemaphoreType.DMA((2,)),
            pltpu.SemaphoreType.DMA((2,)),
            pltpu.SemaphoreType.DMA,
            pltpu.SemaphoreType.DMA,
            pltpu.SemaphoreType.DMA((3, RING - 1)),
            pltpu.SemaphoreType.DMA((3, RING - 1)),
        ],
        compiler_params=pltpu.CompilerParams(
            collective_id=0, has_side_effects=True, vmem_limit_bytes=60 << 20
        ),
    )(
        starts[0],
        w_embed,
        pos_embed,
        mod_table.transpose(1, 0, 2),
        mod_index,
        w_qkv.transpose(1, 0, 2),
        w_out,
        text,
        w_final.T,
    )
    return corrected[None], first_velocity[None]


def solution(mesh):
    placed = (
        P("tm", None, "seq"),
        P(),
        P(),
        P(),
        P("tm", None),
        P(None, None, "seq"),
        P("seq", None),
        P(None, None, "seq"),
        P(),
    )
    return jax.shard_map(
        on_device,
        mesh=mesh,
        in_specs=placed,
        out_specs=(P("tm", None, "seq"), P("tm", None, "seq")),
        check_vma=False,
    )
```

```python
import functools
import math

import jax
import jax.numpy as jnp
from jax import lax
from jax.experimental import pallas as pl
from jax.experimental.pallas import tpu as pltpu
from jax.sharding import PartitionSpec as P

HD = 64
MESH = pl.DeviceIdType.MESH
F32 = jnp.float32
BF16 = jnp.bfloat16
TN = (((0,), (0,)), ((), ()))
NT = (((1,), (1,)), ((), ()))
RING = 4
EXTRA = 16


def moment(step_index, step_total):
    shifted = 1.0 - 0.95 * step_index.astype(F32) / step_total
    return 3.0 * shifted / (1.0 + 2.0 * shifted)


def split_rows(row):
    parts = []
    for _ in range(3):
        part = row.astype(BF16).astype(F32)
        parts.append(part)
        row = row - part
    parts.append(jnp.zeros((EXTRA - 3, row.shape[1]), F32))
    return jnp.concatenate(parts, axis=0).astype(BF16)


def span(index, size, align):
    return pl.ds(pl.multiple_of(index * size, align), size)


def kernel(
    key_total,
    starts,
    w_embed_hbm,
    pos_hbm,
    mod_table_hbm,
    mod_index,
    w_qkv_hbm,
    w_out_hbm,
    text_hbm,
    w_final_hbm,
    corrected,
    first_velocity,
    w_embed,
    w_embed_t,
    w_sums,
    pos,
    pos_t,
    pos_sums,
    hidden,
    work,
    mod_table,
    gate_t,
    w_qkv,
    w_out,
    w_out_t,
    text,
    w_final,
    latents,
    state,
    modulated,
    queries,
    keys,
    values,
    scores_a,
    scores_b,
    attended,
    sums_out,
    sums_in,
    load_sem,
    ready_sem,
    latent_send,
    latent_recv,
    att_send,
    att_recv,
    wide_send,
    wide_recv,
    scan_send,
    scan_recv,
):
    own_block = lax.axis_index("tm")
    own = lax.axis_index("seq")
    blocks = lax.axis_size("tm")
    peer = {"tm": own_block, "seq": 1 - own}
    channels, share = starts.shape
    image = 2 * share
    head_cols = w_out_hbm.shape[0]
    heads = head_cols // HD
    fine_steps = mod_index.shape[1]
    step_total = blocks * fine_steps
    own_tokens = span(own, share, share)

    ring_axes = []
    for stride in (1, RING, RING * RING):
        place = (own_block // stride) % RING
        peers = []
        for distance in range(1, RING):
            target = own_block + ((place + distance) % RING - place) * stride
            peers.append({"tm": target, "seq": own})
        ring_axes.append((place, peers))

    barrier = pltpu.get_barrier_semaphore()
    pl.semaphore_signal(barrier, inc=1, device_id=peer, device_id_type=MESH)

    def for_peers(higher, action):
        for place, peers in ring_axes:
            for distance, device in enumerate(peers, 1):
                above = place + distance < RING

                @pl.when(above if higher else jnp.logical_not(above))
                def _():
                    action(device)

    def greet(device):
        pl.semaphore_signal(barrier, inc=1, device_id=device, device_id_type=MESH)

    def answer(device):
        pl.semaphore_signal(ready_sem, inc=1, device_id=device, device_id_type=MESH)

    for_peers(True, greet)
    below = sum([place for place, _ in ring_axes], jnp.int32(0))
    above_total = (RING - 1) * len(ring_axes) - below

    chunk = 256
    chunks = image // chunk
    half = chunks // 2
    width = pos.shape[1]
    third = -(-width // 48) * 16
    out_cuts = [0, third, 2 * third, width]

    def ordered(index):
        return span((own * half + index) % chunks, chunk, chunk)

    def load(source, target, index):
        copy = pltpu.make_async_copy(source, target, load_sem.at[index])
        return copy

    embed_loads = [load(w_embed_hbm, w_embed.at[:channels, :], 0), load(mod_table_hbm, mod_table, 1)]
    pos_loads = [
        load(pos_hbm.at[ordered(index), :], pos.at[ordered(index), :], 2 + index)
        for index in range(chunks)
    ]
    out_loads = [load(w_out_hbm, w_out, 6), load(text_hbm, text, 7), load(w_final_hbm, w_final, 8)]
    qkv_loads = [load(w_qkv_hbm.at[part], w_qkv.at[part], 9 + part) for part in range(3)]
    for copy in embed_loads + pos_loads + out_loads + qkv_loads:
        copy.start()

    state[...] = starts[...]
    latents[0, :, own_tokens] = starts[...].astype(BF16)
    pl.semaphore_wait(barrier, 1 + below)
    for_peers(False, answer)

    def latent_copy(step):
        return pltpu.make_async_remote_copy(
            src_ref=latents.at[step, :, own_tokens],
            dst_ref=latents.at[step, :, own_tokens],
            send_sem=latent_send.at[step],
            recv_sem=latent_recv.at[step],
            device_id=peer,
            device_id_type=MESH,
        )

    def attended_copy(step):
        return pltpu.make_async_remote_copy(
            src_ref=attended.at[:head_cols],
            dst_ref=attended.at[2 * head_cols :],
            send_sem=att_send.at[step],
            recv_sem=att_recv.at[step],
            device_id=peer,
            device_id_type=MESH,
        )

    latent_copy(0).start()
    wide_copy = pltpu.make_async_remote_copy(
        src_ref=w_out_t.at[:, :head_cols],
        dst_ref=w_out_t.at[:, head_cols:],
        send_sem=wide_send,
        recv_sem=wide_recv,
        device_id=peer,
        device_id_type=MESH,
    )
    for copy in embed_loads:
        copy.wait()
    w_embed_t[...] = w_embed[:channels, :].T
    w_embed[channels:, :] = jnp.ones((EXTRA, width), BF16)
    w_sums[...] = jnp.broadcast_to(
        jnp.sum(w_embed[:channels, :].astype(F32), axis=1, keepdims=True), (channels, 128)
    )

    lane = lax.broadcasted_iota(jnp.int32, (1, 2 * HD), 1)
    key_row = lax.broadcasted_iota(jnp.int32, (8, 1), 0)
    key_rows = keys.shape[0]

    def score(index, buffer):
        index = jnp.minimum(index, 2 * heads - 1)
        tile = jnp.where(index < heads, 1 - own, own)
        head = index % heads
        pair = span(head // 2, 2 * HD, 2 * HD)
        query = queries[span(tile, share, share), pair]
        query = jnp.where(lane // HD == head % 2, query, jnp.zeros_like(query))
        buffer[...] = lax.dot_general(keys[:, pair], query, NT, preferred_element_type=F32)
        buffer[key_rows - 8 :, :] = jnp.where(
            key_row < key_total - (key_rows - 8), buffer[key_rows - 8 :, :], -1e30
        )

    def attend(index, buffer):
        head = index % heads
        rows = span(head, HD, HD)
        value = buffer[...]
        expanded = jnp.exp2(value - jnp.max(value, axis=0, keepdims=True))
        total = jnp.sum(expanded, axis=0, keepdims=True)
        result = jnp.dot(values[rows, :], expanded.astype(BF16), preferred_element_type=F32)
        attended[span(index, HD, HD), :] = (result / total).astype(BF16)

    def fine_step(step, carry):
        level = mod_index[0, step]
        shift = mod_table[0, pl.ds(level, 1), :]
        scale = 1.0 + mod_table[1, pl.ds(level, 1), :]
        gate = mod_table[2, pl.ds(level, 1), :]

        def modulate(index, carry):
            @pl.when(step == 0)
            def _():
                for place in range(chunks):

                    @pl.when(index == place)
                    def _():
                        pos_loads[place].wait()

            @pl.when(index == half)
            def _():
                latent_copy(step).wait_recv()

            tokens = ordered(index)
            @pl.when(step == 0)
            def _():
                ones = jnp.ones((EXTRA, width), BF16)
                pos_sums[:, tokens] = lax.dot_general(
                    ones, pos[tokens, :], NT, preferred_element_type=F32
                )[:8]

            latent = latents[step, :, tokens]
            weight = jnp.concatenate([w_sums[...]] * (chunk // 128), axis=1)
            total = jnp.sum(latent.astype(F32) * weight, axis=0, keepdims=True)
            row_mean = (total + pos_sums[:1, tokens]) * (1.0 / width)
            work[...] = lax.dot_general(
                jnp.concatenate([latent, split_rows(-row_mean)], axis=0),
                w_embed[...],
                TN,
                preferred_element_type=F32,
            ) + pos[tokens, :].astype(F32)
            variance = jnp.mean(work[...] * work[...], axis=-1, keepdims=True)
            modulated[tokens, :] = (
                work[...] * lax.rsqrt(variance + 1e-06) * scale + shift
            ).astype(BF16)
            return carry

        lax.fori_loop(0, chunks, modulate, 0)
        latent_copy(step).wait_send()
        gate_t[...] = jnp.broadcast_to(gate, (128, width)).T

        @pl.when(step == 0)
        def _():
            for copy in out_loads:
                copy.wait()
            w_out_t[:, :head_cols] = w_out[...].T
            wide_copy.start()
            pos_t[...] = pos[own_tokens, :].T
            spare = key_rows - key_total
            both = text[...].astype(F32)
            blank = jnp.zeros((spare, head_cols), F32)
            keys[image:, :] = jnp.concatenate([both[:, 0, :], blank], axis=0).astype(BF16)
            value_rows = jnp.concatenate([both[:, 1, :], blank], axis=0).astype(BF16)
            values[:, image:] = value_rows.T
            for copy in qkv_loads:
                copy.wait()

        def project(part):
            return jnp.dot(modulated[...], w_qkv[part], preferred_element_type=F32)

        queries[...] = (project(0) * (HD**-0.5 / math.log(2))).astype(BF16)
        keys[:image, :] = project(1).astype(BF16)
        values[:, :image] = project(2).astype(BF16).T

        score(0, scores_a)

        def pair_of_heads(index, carry):
            score(2 * index + 1, scores_b)
            attend(2 * index, scores_a)
            score(2 * index + 2, scores_a)
            attend(2 * index + 1, scores_b)
            return carry

        lax.fori_loop(0, heads // 2, pair_of_heads, 0)
        attended_copy(step).start()
        lax.fori_loop(heads // 2, heads, pair_of_heads, 0)
        attended_copy(step).wait()

        @pl.when(step == 0)
        def _():
            wide_copy.wait()

        fine_index = own_block * fine_steps + step
        pace = moment(fine_index + 1, step_total) - moment(fine_index, step_total)

        gates = jnp.concatenate([gate_t[...]] * (share // 128), axis=1)
        middle = None
        first = jnp.zeros((1, share), F32)
        second = jnp.zeros((1, share), F32)
        for low, high in zip(out_cuts[:-1], out_cuts[1:]):
            rows = slice(low, high)
            mixed = jnp.dot(
                w_out_t[rows, :], attended[head_cols:, :], preferred_element_type=F32
            )
            embedded = jnp.dot(
                w_embed_t[rows, :], latents[step, :, own_tokens], preferred_element_type=F32
            )
            part = embedded + pos_t[rows, :].astype(F32) + gates[rows, :] * mixed
            hidden[rows, :] = part
            if middle is None:
                middle = jnp.mean(part, axis=0, keepdims=True)
            moved = hidden[rows, :] - middle
            first = first + jnp.sum(moved, axis=0, keepdims=True)
            second = second + jnp.sum(moved * moved, axis=0, keepdims=True)
        first = first * (1.0 / width)
        spread = lax.rsqrt(second * (1.0 / width) - first * first + 1e-06)
        normed = ((hidden[...] - (middle + first)) * spread).astype(BF16)
        speed = jnp.dot(w_final[...], normed, preferred_element_type=F32)
        state[...] = state[...] + pace * speed

        @pl.when(step == 0)
        def _():
            first_velocity[...] = speed

        @pl.when(step < fine_steps - 1)
        def _():
            latents[step + 1, :, own_tokens] = state[...].astype(BF16)
            latent_copy(step + 1).start()

        return carry

    lax.fori_loop(0, fine_steps, fine_step, 0)

    time_before = moment(own_block * fine_steps, step_total)
    time_after = moment((own_block + 1) * fine_steps, step_total)
    keep_start = jnp.where(own_block == 0, 0.0, 1.0)
    share_sum = state[...] / time_after - (keep_start / time_before) * starts[...]
    result = share_sum

    @pl.when(above_total > 0)
    def _():
        pl.semaphore_wait(ready_sem, above_total)

    for axis, (place, peers) in enumerate(ring_axes):
        upward = axis == len(ring_axes) - 1
        sums_out[axis] = share_sum.astype(BF16)
        copies = []
        for slot, device in enumerate(peers):
            copy = pltpu.make_async_remote_copy(
                src_ref=sums_out.at[axis],
                dst_ref=sums_in.at[axis, slot],
                send_sem=scan_send.at[axis, slot],
                recv_sem=scan_recv.at[axis, slot],
                device_id=device,
                device_id_type=MESH,
            )
            copies.append(copy)
            if upward:
                pl.when(place + slot + 1 < RING)(copy.start)
            else:
                copy.start()
        if upward:
            corrected[...] = result
        for slot, copy in enumerate(copies):
            if upward:

                @pl.when(place >= slot + 1)
                def _():
                    copy.wait_recv()
                    corrected[...] += sums_in[axis, slot].astype(F32)

            else:
                copy.wait()
                arrived = sums_in[axis, slot].astype(F32)
                earlier = jnp.where(place >= slot + 1, 1.0, 0.0)
                result = result + earlier * arrived
                share_sum = share_sum + arrived
        if upward:
            for slot, copy in enumerate(copies):
                pl.when(place + slot + 1 < RING)(copy.wait_send)
    corrected[...] = time_after * corrected[...]


def hand_over(corrected, first_velocity, corrected_out, first_velocity_out):
    corrected_out[0] = corrected[...]
    first_velocity_out[0] = first_velocity[...]


def on_device(starts, w_embed, pos_embed, mod_table, mod_index, w_qkv, w_out, text_kv, w_final):
    channels, share = starts.shape[1:]
    image, width = pos_embed.shape
    head_cols = w_out.shape[0]
    text_total = text_kv.shape[1]
    text_rows = -(-text_total // 16) * 16
    key_rows = image + text_rows
    text = text_kv.transpose(1, 0, 2)
    vmem = pl.BlockSpec(memory_space=pltpu.VMEM)
    anywhere = pl.BlockSpec(memory_space=pl.ANY)
    corrected, first_velocity = pl.pallas_call(
        functools.partial(kernel, image + text_total),
        out_shape=[jax.ShapeDtypeStruct((channels, share), F32)] * 2,
        in_specs=[
            vmem,
            anywhere,
            anywhere,
            anywhere,
            pl.BlockSpec(memory_space=pltpu.SMEM),
            anywhere,
            anywhere,
            anywhere,
            anywhere,
        ],
        out_specs=[vmem, vmem],
        scratch_shapes=[
            pltpu.VMEM((channels + EXTRA, width), BF16),
            pltpu.VMEM((width, channels), BF16),
            pltpu.VMEM((channels, 128), F32),
            pltpu.VMEM((image, width), BF16),
            pltpu.VMEM((width, share), BF16),
            pltpu.VMEM((8, image), F32),
            pltpu.VMEM((width, share), F32),
            pltpu.VMEM((256, width), F32),
            pltpu.VMEM((3, mod_table.shape[0], width), F32),
            pltpu.VMEM((width, 128), F32),
            pltpu.VMEM((3, width, head_cols), BF16),
            pltpu.VMEM((head_cols, width), BF16),
            pltpu.VMEM((width, 2 * head_cols), BF16),
            pltpu.VMEM((text_total, 2, head_cols), BF16),
            pltpu.VMEM((channels, width), BF16),
            pltpu.VMEM((2, channels, image), BF16),
            pltpu.VMEM((channels, share), F32),
            pltpu.VMEM((image, width), BF16),
            pltpu.VMEM((image, head_cols), BF16),
            pltpu.VMEM((key_rows, head_cols), BF16),
            pltpu.VMEM((head_cols, key_rows), BF16),
            pltpu.VMEM((key_rows, share), F32),
            pltpu.VMEM((key_rows, share), F32),
            pltpu.VMEM((3 * head_cols, share), BF16),
            pltpu.VMEM((3, channels, share), BF16),
            pltpu.VMEM((3, RING - 1, channels, share), BF16),
            pltpu.SemaphoreType.DMA((12,)),
            pltpu.SemaphoreType.REGULAR,
            pltpu.SemaphoreType.DMA((2,)),
            pltpu.SemaphoreType.DMA((2,)),
            pltpu.SemaphoreType.DMA((2,)),
            pltpu.SemaphoreType.DMA((2,)),
            pltpu.SemaphoreType.DMA,
            pltpu.SemaphoreType.DMA,
            pltpu.SemaphoreType.DMA((3, RING - 1)),
            pltpu.SemaphoreType.DMA((3, RING - 1)),
        ],
        compiler_params=pltpu.CompilerParams(
            collective_id=0, has_side_effects=True, vmem_limit_bytes=62 << 20
        ),
    )(
        starts[0],
        w_embed,
        pos_embed,
        mod_table.transpose(1, 0, 2),
        mod_index,
        w_qkv.transpose(1, 0, 2),
        w_out,
        text,
        w_final.T,
    )
    shape = jax.ShapeDtypeStruct((1, channels, share), F32)
    return pl.pallas_call(
        hand_over,
        out_shape=[shape] * 2,
        in_specs=[vmem, vmem],
        out_specs=[vmem, vmem],
    )(corrected, first_velocity)


def solution(mesh):
    placed = (
        P("tm", None, "seq"),
        P(),
        P(),
        P(),
        P("tm", None),
        P(None, None, "seq"),
        P("seq", None),
        P(None, None, "seq"),
        P(),
    )
    return jax.shard_map(
        on_device,
        mesh=mesh,
        in_specs=placed,
        out_specs=(P("tm", None, "seq"), P("tm", None, "seq")),
        check_vma=False,
    )
```

```python
import functools
import math

import jax
import jax.numpy as jnp
from jax import lax
from jax.experimental import pallas as pl
from jax.experimental.pallas import tpu as pltpu
from jax.sharding import PartitionSpec as P

HD = 64
MESH = pl.DeviceIdType.MESH
F32 = jnp.float32
BF16 = jnp.bfloat16
TN = (((0,), (0,)), ((), ()))
NT = (((1,), (1,)), ((), ()))
RING = 4
EXTRA = 16


def moment(step_index, step_total):
    shifted = 1.0 - 0.95 * step_index.astype(F32) / step_total
    return 3.0 * shifted / (1.0 + 2.0 * shifted)


def split_rows(row):
    parts = []
    for _ in range(3):
        part = row.astype(BF16).astype(F32)
        parts.append(part)
        row = row - part
    parts.append(jnp.zeros((EXTRA - 3, row.shape[1]), F32))
    return jnp.concatenate(parts, axis=0).astype(BF16)


def span(index, size, align):
    return pl.ds(pl.multiple_of(index * size, align), size)


def kernel(
    key_total,
    starts,
    w_embed_hbm,
    pos_hbm,
    mod_table_hbm,
    mod_index,
    w_qkv_hbm,
    w_out_hbm,
    text_hbm,
    w_final_hbm,
    corrected,
    first_velocity,
    w_embed,
    w_embed_t,
    w_sums,
    pos,
    pos_t,
    pos_sums,
    hidden,
    mod_table,
    gate_t,
    w_qkv,
    w_out,
    w_out_t,
    text,
    w_final,
    latents,
    state,
    modulated,
    queries,
    keys,
    values,
    scores_a,
    scores_b,
    attended,
    sums_out,
    sums_in,
    load_sem,
    ready_sem,
    latent_send,
    latent_recv,
    att_send,
    att_recv,
    wide_send,
    wide_recv,
    scan_send,
    scan_recv,
):
    own_block = lax.axis_index("tm")
    own = lax.axis_index("seq")
    blocks = lax.axis_size("tm")
    peer = {"tm": own_block, "seq": 1 - own}
    channels, share = starts.shape
    image = 2 * share
    head_cols = w_out_hbm.shape[0]
    heads = head_cols // HD
    fine_steps = mod_index.shape[1]
    step_total = blocks * fine_steps
    own_tokens = span(own, share, share)

    ring_axes = []
    for stride in (1, RING, RING * RING):
        place = (own_block // stride) % RING
        peers = []
        for distance in range(1, RING):
            target = own_block + ((place + distance) % RING - place) * stride
            peers.append({"tm": target, "seq": own})
        ring_axes.append((place, peers))

    barrier = pltpu.get_barrier_semaphore()
    pl.semaphore_signal(barrier, inc=1, device_id=peer, device_id_type=MESH)

    def for_peers(higher, action):
        for place, peers in ring_axes:
            for distance, device in enumerate(peers, 1):
                above = place + distance < RING

                @pl.when(above if higher else jnp.logical_not(above))
                def _():
                    action(device)

    def greet(device):
        pl.semaphore_signal(barrier, inc=1, device_id=device, device_id_type=MESH)

    def answer(device):
        pl.semaphore_signal(ready_sem, inc=1, device_id=device, device_id_type=MESH)

    for_peers(True, greet)
    below = sum([place for place, _ in ring_axes], jnp.int32(0))
    above_total = (RING - 1) * len(ring_axes) - below

    chunk = 256
    chunks = image // chunk
    half = chunks // 2
    width = pos.shape[1]
    third = -(-width // 48) * 16
    out_cuts = [0, third, 2 * third, width]

    def ordered(index):
        return span((own * half + index) % chunks, chunk, chunk)

    def load(source, target, index):
        copy = pltpu.make_async_copy(source, target, load_sem.at[index])
        return copy

    embed_loads = [load(w_embed_hbm, w_embed.at[:channels, :], 0), load(mod_table_hbm, mod_table, 1)]
    pos_loads = [
        load(pos_hbm.at[ordered(index), :], pos.at[ordered(index), :], 2 + index)
        for index in range(chunks)
    ]
    out_loads = [load(w_out_hbm, w_out, 6), load(text_hbm, text, 7), load(w_final_hbm, w_final, 8)]
    qkv_loads = [load(w_qkv_hbm.at[part], w_qkv.at[part], 9 + part) for part in range(3)]
    for copy in embed_loads + pos_loads + out_loads + qkv_loads:
        copy.start()

    state[...] = starts[...]
    latents[0, :, own_tokens] = starts[...].astype(BF16)
    pl.semaphore_wait(barrier, 1 + below)
    for_peers(False, answer)

    def latent_copy(step):
        return pltpu.make_async_remote_copy(
            src_ref=latents.at[step, :, own_tokens],
            dst_ref=latents.at[step, :, own_tokens],
            send_sem=latent_send.at[step],
            recv_sem=latent_recv.at[step],
            device_id=peer,
            device_id_type=MESH,
        )

    def attended_copy(step):
        return pltpu.make_async_remote_copy(
            src_ref=attended.at[:head_cols],
            dst_ref=attended.at[2 * head_cols :],
            send_sem=att_send.at[step],
            recv_sem=att_recv.at[step],
            device_id=peer,
            device_id_type=MESH,
        )

    latent_copy(0).start()
    wide_copy = pltpu.make_async_remote_copy(
        src_ref=w_out_t.at[:, :head_cols],
        dst_ref=w_out_t.at[:, head_cols:],
        send_sem=wide_send,
        recv_sem=wide_recv,
        device_id=peer,
        device_id_type=MESH,
    )
    for copy in embed_loads:
        copy.wait()
    w_embed_t[...] = w_embed[:channels, :].T
    w_embed[channels:, :] = jnp.ones((EXTRA, width), BF16)
    w_sums[...] = jnp.broadcast_to(
        jnp.sum(w_embed[:channels, :].astype(F32), axis=1, keepdims=True), (channels, 128)
    )

    feature = lax.broadcasted_iota(jnp.int32, (2 * HD, 1), 0)
    key_row = lax.broadcasted_iota(jnp.int32, (8, 1), 0)
    key_rows = keys.shape[0]

    def score(index, buffer):
        tile = jnp.where(index < heads, 1 - own, own)
        head = index % heads
        pair = span(head // 2, 2 * HD, 2 * HD)
        query = queries[pair, span(tile, share, share)]
        query = jnp.where(feature // HD == head % 2, query, jnp.zeros_like(query))
        buffer[...] = jnp.dot(keys[:, pair], query, preferred_element_type=F32)
        buffer[key_rows - 8 :, :] = jnp.where(
            key_row < key_total - (key_rows - 8), buffer[key_rows - 8 :, :], -1e30
        )

    def attend(index, buffer):
        head = index % heads
        rows = span(head, HD, HD)
        value = buffer[...]
        expanded = jnp.exp2(value - jnp.max(value, axis=0, keepdims=True))
        weights = jnp.concatenate([values[rows, :], jnp.ones((EXTRA, key_rows), BF16)], axis=0)
        result = jnp.dot(weights, expanded.astype(BF16), preferred_element_type=F32)
        total = result[HD : HD + 1]
        result = result[:HD]
        attended[span(index, HD, HD), :] = (result / total).astype(BF16)

    def fine_step(step, carry):
        level = mod_index[0, step]
        shift = mod_table[0, pl.ds(level, 1), :]
        scale = 1.0 + mod_table[1, pl.ds(level, 1), :]
        gate = mod_table[2, pl.ds(level, 1), :]

        def modulate(index, carry):
            @pl.when(step == 0)
            def _():
                for place in range(chunks):

                    @pl.when(index == place)
                    def _():
                        pos_loads[place].wait()

            @pl.when(index == half)
            def _():
                latent_copy(step).wait_recv()

            tokens = ordered(index)
            @pl.when(step == 0)
            def _():
                ones = jnp.ones((EXTRA, width), BF16)
                pos_sums[:, tokens] = lax.dot_general(
                    ones, pos[tokens, :], NT, preferred_element_type=F32
                )[:8]

            latent = latents[step, :, tokens]
            weight = jnp.concatenate([w_sums[...]] * (chunk // 128), axis=1)
            total = jnp.sum(latent.astype(F32) * weight, axis=0, keepdims=True)
            row_mean = (total + pos_sums[:1, tokens]) * (1.0 / width)
            centered = lax.dot_general(
                jnp.concatenate([latent, split_rows(-row_mean)], axis=0),
                w_embed[...],
                TN,
                preferred_element_type=F32,
            ) + pos[tokens, :].astype(F32)
            variance = jnp.mean(centered * centered, axis=-1, keepdims=True)
            modulated[tokens, :] = (
                centered * lax.rsqrt(variance + 1e-06) * scale + shift
            ).astype(BF16)
            return carry

        lax.fori_loop(0, chunks, modulate, 0)
        latent_copy(step).wait_send()
        gate_t[...] = jnp.broadcast_to(gate, (128, width)).T

        @pl.when(step == 0)
        def _():
            for copy in out_loads:
                copy.wait()
            w_out_t[:, :head_cols] = w_out[...].T
            wide_copy.start()
            pos_t[...] = pos[own_tokens, :].T
            spare = key_rows - key_total
            both = text[...].astype(F32)
            blank = jnp.zeros((spare, head_cols), F32)
            keys[image:, :] = jnp.concatenate([both[:, 0, :], blank], axis=0).astype(BF16)
            value_rows = jnp.concatenate([both[:, 1, :], blank], axis=0).astype(BF16)
            values[:, image:] = value_rows.T
            for copy in qkv_loads:
                copy.wait()

        def project(part):
            return jnp.dot(modulated[...], w_qkv[part], preferred_element_type=F32)

        queries[...] = (project(0) * (HD**-0.5 / math.log(2))).astype(BF16).T
        keys[:image, :] = project(1).astype(BF16)
        values[:, :image] = project(2).astype(BF16).T

        score(0, scores_a)

        def pair_of_heads(index, carry):
            score(2 * index + 1, scores_b)
            attend(2 * index, scores_a)
            score(2 * index + 2, scores_a)
            attend(2 * index + 1, scores_b)
            return carry

        lax.fori_loop(0, heads // 2, pair_of_heads, 0, unroll=3)
        attended_copy(step).start()
        lax.fori_loop(heads // 2, heads - 3, pair_of_heads, 0, unroll=3)
        for index in range(heads - 3, heads - 1):
            pair_of_heads(index, 0)
        score(2 * heads - 1, scores_b)
        attend(2 * heads - 2, scores_a)
        attend(2 * heads - 1, scores_b)
        attended_copy(step).wait()

        @pl.when(step == 0)
        def _():
            wide_copy.wait()

        fine_index = own_block * fine_steps + step
        pace = moment(fine_index + 1, step_total) - moment(fine_index, step_total)

        gates = jnp.concatenate([gate_t[...]] * (share // 128), axis=1)
        middle = None
        first = jnp.zeros((1, share), F32)
        second = jnp.zeros((1, share), F32)
        for low, high in zip(out_cuts[:-1], out_cuts[1:]):
            rows = slice(low, high)
            mixed = jnp.dot(
                w_out_t[rows, :], attended[head_cols:, :], preferred_element_type=F32
            )
            embedded = jnp.dot(
                w_embed_t[rows, :], latents[step, :, own_tokens], preferred_element_type=F32
            )
            part = embedded + pos_t[rows, :].astype(F32) + gates[rows, :] * mixed
            hidden[rows, :] = part
            if middle is None:
                middle = jnp.mean(part, axis=0, keepdims=True)
            moved = hidden[rows, :] - middle
            first = first + jnp.sum(moved, axis=0, keepdims=True)
            second = second + jnp.sum(moved * moved, axis=0, keepdims=True)
        first = first * (1.0 / width)
        spread = lax.rsqrt(second * (1.0 / width) - first * first + 1e-06)
        normed = ((hidden[...] - (middle + first)) * spread).astype(BF16)
        speed = jnp.dot(w_final[...], normed, preferred_element_type=F32)
        state[...] = state[...] + pace * speed

        @pl.when(step == 0)
        def _():
            first_velocity[...] = speed

        @pl.when(step < fine_steps - 1)
        def _():
            latents[step + 1, :, own_tokens] = state[...].astype(BF16)
            latent_copy(step + 1).start()

        return carry

    lax.fori_loop(0, fine_steps, fine_step, 0)

    time_before = moment(own_block * fine_steps, step_total)
    time_after = moment((own_block + 1) * fine_steps, step_total)
    keep_start = jnp.where(own_block == 0, 0.0, 1.0)
    share_sum = state[...] / time_after - (keep_start / time_before) * starts[...]
    result = share_sum

    @pl.when(above_total > 0)
    def _():
        pl.semaphore_wait(ready_sem, above_total)

    for axis, (place, peers) in enumerate(ring_axes):
        upward = axis == len(ring_axes) - 1
        sums_out[...] = share_sum.astype(BF16)
        copies = []
        for slot, device in enumerate(peers):
            copy = pltpu.make_async_remote_copy(
                src_ref=sums_out,
                dst_ref=sums_in.at[axis, slot],
                send_sem=scan_send.at[axis, slot],
                recv_sem=scan_recv.at[axis, slot],
                device_id=device,
                device_id_type=MESH,
            )
            copies.append(copy)
            if upward:
                pl.when(place + slot + 1 < RING)(copy.start)
            else:
                copy.start()
        if upward:
            corrected[...] = result
        for slot, copy in enumerate(copies):
            if upward:

                @pl.when(place >= slot + 1)
                def _():
                    copy.wait_recv()
                    corrected[...] += sums_in[axis, slot].astype(F32)

            else:
                copy.wait()
                arrived = sums_in[axis, slot].astype(F32)
                earlier = jnp.where(place >= slot + 1, 1.0, 0.0)
                result = result + earlier * arrived
                share_sum = share_sum + arrived
        if upward:
            for slot, copy in enumerate(copies):
                pl.when(place + slot + 1 < RING)(copy.wait_send)
    corrected[...] = time_after * corrected[...]


def hand_over(corrected, first_velocity, corrected_out, first_velocity_out):
    corrected_out[0] = corrected[...]
    first_velocity_out[0] = first_velocity[...]


def on_device(starts, w_embed, pos_embed, mod_table, mod_index, w_qkv, w_out, text_kv, w_final):
    channels, share = starts.shape[1:]
    image, width = pos_embed.shape
    head_cols = w_out.shape[0]
    text_total = text_kv.shape[1]
    text_rows = -(-text_total // 16) * 16
    key_rows = image + text_rows
    text = text_kv.transpose(1, 0, 2)
    vmem = pl.BlockSpec(memory_space=pltpu.VMEM)
    anywhere = pl.BlockSpec(memory_space=pl.ANY)
    corrected, first_velocity = pl.pallas_call(
        functools.partial(kernel, image + text_total),
        out_shape=[jax.ShapeDtypeStruct((channels, share), F32)] * 2,
        in_specs=[
            vmem,
            anywhere,
            anywhere,
            anywhere,
            pl.BlockSpec(memory_space=pltpu.SMEM),
            anywhere,
            anywhere,
            anywhere,
            anywhere,
        ],
        out_specs=[vmem, vmem],
        scratch_shapes=[
            pltpu.VMEM((channels + EXTRA, width), BF16),
            pltpu.VMEM((width, channels), BF16),
            pltpu.VMEM((channels, 128), F32),
            pltpu.VMEM((image, width), BF16),
            pltpu.VMEM((width, share), BF16),
            pltpu.VMEM((8, image), F32),
            pltpu.VMEM((width, share), F32),
            pltpu.VMEM((3, mod_table.shape[0], width), F32),
            pltpu.VMEM((width, 128), F32),
            pltpu.VMEM((3, width, head_cols), BF16),
            pltpu.VMEM((head_cols, width), BF16),
            pltpu.VMEM((width, 2 * head_cols), BF16),
            pltpu.VMEM((text_total, 2, head_cols), BF16),
            pltpu.VMEM((channels, width), BF16),
            pltpu.VMEM((2, channels, image), BF16),
            pltpu.VMEM((channels, share), F32),
            pltpu.VMEM((image, width), BF16),
            pltpu.VMEM((head_cols, image), BF16),
            pltpu.VMEM((key_rows, head_cols), BF16),
            pltpu.VMEM((head_cols, key_rows), BF16),
            pltpu.VMEM((key_rows, share), F32),
            pltpu.VMEM((key_rows, share), F32),
            pltpu.VMEM((3 * head_cols, share), BF16),
            pltpu.VMEM((channels, share), BF16),
            pltpu.VMEM((3, RING - 1, channels, share), BF16),
            pltpu.SemaphoreType.DMA((12,)),
            pltpu.SemaphoreType.REGULAR,
            pltpu.SemaphoreType.DMA((2,)),
            pltpu.SemaphoreType.DMA((2,)),
            pltpu.SemaphoreType.DMA((2,)),
            pltpu.SemaphoreType.DMA((2,)),
            pltpu.SemaphoreType.DMA,
            pltpu.SemaphoreType.DMA,
            pltpu.SemaphoreType.DMA((3, RING - 1)),
            pltpu.SemaphoreType.DMA((3, RING - 1)),
        ],
        compiler_params=pltpu.CompilerParams(
            collective_id=0, has_side_effects=True, vmem_limit_bytes=63 << 20
        ),
    )(
        starts[0],
        w_embed,
        pos_embed,
        mod_table.transpose(1, 0, 2),
        mod_index,
        w_qkv.transpose(1, 0, 2),
        w_out,
        text,
        w_final.T,
    )
    shape = jax.ShapeDtypeStruct((1, channels, share), F32)
    return pl.pallas_call(
        hand_over,
        out_shape=[shape] * 2,
        in_specs=[vmem, vmem],
        out_specs=[vmem, vmem],
    )(corrected, first_velocity)


def solution(mesh):
    placed = (
        P("tm", None, "seq"),
        P(),
        P(),
        P(),
        P("tm", None),
        P(None, None, "seq"),
        P("seq", None),
        P(None, None, "seq"),
        P(),
    )
    return jax.shard_map(
        on_device,
        mesh=mesh,
        in_specs=placed,
        out_specs=(P("tm", None, "seq"), P("tm", None, "seq")),
        check_vma=False,
    )
```

```python
import functools
import math

import jax
import jax.numpy as jnp
from jax import lax
from jax.experimental import pallas as pl
from jax.experimental.pallas import tpu as pltpu
from jax.sharding import PartitionSpec as P

HD = 64
MESH = pl.DeviceIdType.MESH
F32 = jnp.float32
BF16 = jnp.bfloat16
TN = (((0,), (0,)), ((), ()))
NT = (((1,), (1,)), ((), ()))
RING = 4
EXTRA = 16


def moment(step_index, step_total):
    shifted = 1.0 - 0.95 * step_index.astype(F32) / step_total
    return 3.0 * shifted / (1.0 + 2.0 * shifted)


def split_rows(row):
    parts = []
    for _ in range(3):
        part = row.astype(BF16).astype(F32)
        parts.append(part)
        row = row - part
    parts.append(jnp.zeros((EXTRA - 3, row.shape[1]), F32))
    return jnp.concatenate(parts, axis=0).astype(BF16)


def span(index, size, align):
    return pl.ds(pl.multiple_of(index * size, align), size)


def kernel(
    key_total,
    starts,
    w_embed_hbm,
    pos_hbm,
    mod_table_hbm,
    mod_index,
    w_qkv_hbm,
    w_out_hbm,
    text_hbm,
    w_final_hbm,
    corrected,
    first_velocity,
    w_embed,
    w_embed_t,
    w_sums,
    pos,
    pos_t,
    pos_sums,
    hidden,
    mod_table,
    gate_t,
    w_qkv,
    w_out,
    w_out_t,
    text,
    w_final,
    latents,
    state,
    modulated,
    queries,
    keys,
    values,
    scores_a,
    scores_b,
    attended,
    sums_out,
    sums_in,
    load_sem,
    ready_sem,
    latent_send,
    latent_recv,
    att_send,
    att_recv,
    wide_send,
    wide_recv,
    scan_send,
    scan_recv,
):
    own_block = lax.axis_index("tm")
    own = lax.axis_index("seq")
    blocks = lax.axis_size("tm")
    peer = {"tm": own_block, "seq": 1 - own}
    channels, share = starts.shape
    image = 2 * share
    head_cols = w_out_hbm.shape[0]
    heads = head_cols // HD
    fine_steps = mod_index.shape[1]
    step_total = blocks * fine_steps
    own_tokens = span(own, share, share)

    ring_axes = []
    for stride in (1, RING, RING * RING):
        place = (own_block // stride) % RING
        peers = []
        for distance in range(1, RING):
            target = own_block + ((place + distance) % RING - place) * stride
            peers.append({"tm": target, "seq": own})
        ring_axes.append((place, peers))

    barrier = pltpu.get_barrier_semaphore()
    pl.semaphore_signal(barrier, inc=1, device_id=peer, device_id_type=MESH)

    def for_peers(higher, action):
        for place, peers in ring_axes:
            for distance, device in enumerate(peers, 1):
                above = place + distance < RING

                @pl.when(above if higher else jnp.logical_not(above))
                def _():
                    action(device)

    def greet(device):
        pl.semaphore_signal(barrier, inc=1, device_id=device, device_id_type=MESH)

    def answer(device):
        pl.semaphore_signal(ready_sem, inc=1, device_id=device, device_id_type=MESH)

    for_peers(True, greet)
    below = sum([place for place, _ in ring_axes], jnp.int32(0))
    above_total = (RING - 1) * len(ring_axes) - below

    chunk = 256
    chunks = image // chunk
    half = chunks // 2
    width = pos.shape[1]
    third = -(-width // 48) * 16
    out_cuts = [0, third, 2 * third, width]

    def ordered(index):
        return span((own * half + index) % chunks, chunk, chunk)

    def load(source, target, index):
        copy = pltpu.make_async_copy(source, target, load_sem.at[index])
        return copy

    embed_loads = [load(w_embed_hbm, w_embed.at[:channels, :], 0), load(mod_table_hbm, mod_table, 1)]
    pos_loads = [
        load(pos_hbm.at[ordered(index), :], pos.at[ordered(index), :], 2 + index)
        for index in range(chunks)
    ]
    out_loads = [load(w_out_hbm, w_out, 6), load(text_hbm, text, 7), load(w_final_hbm, w_final, 8)]
    quarter = width // 4
    qkv_loads = [
        load(
            w_qkv_hbm.at[part, pl.ds(piece * quarter, quarter), :],
            w_qkv.at[part, pl.ds(piece * quarter, quarter), :],
            9 + 4 * part + piece,
        )
        for part in range(3)
        for piece in range(4)
    ]
    for copy in embed_loads + pos_loads + out_loads + qkv_loads:
        copy.start()

    state[...] = starts[...]
    latents[0, :, own_tokens] = starts[...].astype(BF16)
    pl.semaphore_wait(barrier, 1 + below)
    for_peers(False, answer)

    def latent_copy(step):
        return pltpu.make_async_remote_copy(
            src_ref=latents.at[step, :, own_tokens],
            dst_ref=latents.at[step, :, own_tokens],
            send_sem=latent_send.at[step],
            recv_sem=latent_recv.at[step],
            device_id=peer,
            device_id_type=MESH,
        )

    def attended_copy(step):
        return pltpu.make_async_remote_copy(
            src_ref=attended.at[:head_cols],
            dst_ref=attended.at[2 * head_cols :],
            send_sem=att_send.at[step],
            recv_sem=att_recv.at[step],
            device_id=peer,
            device_id_type=MESH,
        )

    latent_copy(0).start()
    wide_copy = pltpu.make_async_remote_copy(
        src_ref=w_out_t.at[:, :head_cols],
        dst_ref=w_out_t.at[:, head_cols:],
        send_sem=wide_send,
        recv_sem=wide_recv,
        device_id=peer,
        device_id_type=MESH,
    )
    for copy in embed_loads:
        copy.wait()
    w_embed_t[...] = w_embed[:channels, :].T
    w_embed[channels:, :] = jnp.ones((EXTRA, width), BF16)
    w_sums[...] = jnp.broadcast_to(
        jnp.sum(w_embed[:channels, :].astype(F32), axis=1, keepdims=True), (channels, 128)
    )

    feature = lax.broadcasted_iota(jnp.int32, (2 * HD, 1), 0)
    key_row = lax.broadcasted_iota(jnp.int32, (8, 1), 0)
    key_rows = keys.shape[0]

    def score(index, buffer):
        tile = jnp.where(index < heads, 1 - own, own)
        head = index % heads
        pair = span(head // 2, 2 * HD, 2 * HD)
        query = queries[pair, span(tile, share, share)]
        query = jnp.where(feature // HD == head % 2, query, jnp.zeros_like(query))
        buffer[...] = jnp.dot(keys[:, pair], query, preferred_element_type=F32)
        buffer[key_rows - 8 :, :] = jnp.where(
            key_row < key_total - (key_rows - 8), buffer[key_rows - 8 :, :], -1e30
        )

    def attend(index, buffer):
        head = index % heads
        rows = span(head, HD, HD)
        value = buffer[...]
        expanded = jnp.exp2(value - jnp.max(value, axis=0, keepdims=True))
        weights = jnp.concatenate([values[rows, :], jnp.ones((EXTRA, key_rows), BF16)], axis=0)
        result = jnp.dot(weights, expanded.astype(BF16), preferred_element_type=F32)
        total = result[HD : HD + 1]
        result = result[:HD]
        attended[span(index, HD, HD), :] = (result / total).astype(BF16)

    def fine_step(step, carry):
        level = mod_index[0, step]
        shift = mod_table[0, pl.ds(level, 1), :]
        scale = 1.0 + mod_table[1, pl.ds(level, 1), :]
        gate = mod_table[2, pl.ds(level, 1), :]

        def modulate(index, carry):
            @pl.when(step == 0)
            def _():
                for place in range(chunks):

                    @pl.when(index == place)
                    def _():
                        pos_loads[place].wait()

            @pl.when(index == half)
            def _():
                latent_copy(step).wait_recv()

            tokens = ordered(index)
            @pl.when(step == 0)
            def _():
                ones = jnp.ones((EXTRA, width), BF16)
                pos_sums[:, tokens] = lax.dot_general(
                    ones, pos[tokens, :], NT, preferred_element_type=F32
                )[:8]

            latent = latents[step, :, tokens]
            weight = jnp.concatenate([w_sums[...]] * (chunk // 128), axis=1)
            total = jnp.sum(latent.astype(F32) * weight, axis=0, keepdims=True)
            row_mean = (total + pos_sums[:1, tokens]) * (1.0 / width)
            centered = lax.dot_general(
                jnp.concatenate([latent, split_rows(-row_mean)], axis=0),
                w_embed[...],
                TN,
                preferred_element_type=F32,
            ) + pos[tokens, :].astype(F32)
            variance = jnp.mean(centered * centered, axis=-1, keepdims=True)
            modulated[tokens, :] = (
                centered * lax.rsqrt(variance + 1e-06) * scale + shift
            ).astype(BF16)
            return carry

        lax.fori_loop(0, chunks, modulate, 0)
        latent_copy(step).wait_send()
        gate_t[...] = jnp.broadcast_to(gate, (128, width)).T

        @pl.when(step == 0)
        def _():
            for copy in out_loads:
                copy.wait()
            w_out_t[:, :head_cols] = w_out[...].T
            wide_copy.start()
            pos_t[...] = pos[own_tokens, :].T
            spare = key_rows - key_total
            both = text[...].astype(F32)
            blank = jnp.zeros((spare, head_cols), F32)
            keys[image:, :] = jnp.concatenate([both[:, 0, :], blank], axis=0).astype(BF16)
            value_rows = jnp.concatenate([both[:, 1, :], blank], axis=0).astype(BF16)
            values[:, image:] = value_rows.T
            for copy in qkv_loads:
                copy.wait()

        def project(part):
            return jnp.dot(modulated[...], w_qkv[part], preferred_element_type=F32)

        queries[...] = (project(0) * (HD**-0.5 / math.log(2))).astype(BF16).T
        keys[:image, :] = project(1).astype(BF16)
        values[:, :image] = project(2).astype(BF16).T

        score(0, scores_a)

        def pair_of_heads(index, carry):
            score(2 * index + 1, scores_b)
            attend(2 * index, scores_a)
            score(2 * index + 2, scores_a)
            attend(2 * index + 1, scores_b)
            return carry

        lax.fori_loop(0, heads // 2, pair_of_heads, 0, unroll=3)
        attended_copy(step).start()
        lax.fori_loop(heads // 2, heads - 3, pair_of_heads, 0, unroll=3)
        for index in range(heads - 3, heads - 1):
            pair_of_heads(index, 0)
        score(2 * heads - 1, scores_b)
        attend(2 * heads - 2, scores_a)
        attend(2 * heads - 1, scores_b)
        attended_copy(step).wait()

        @pl.when(step == 0)
        def _():
            wide_copy.wait()

        fine_index = own_block * fine_steps + step
        pace = moment(fine_index + 1, step_total) - moment(fine_index, step_total)

        gates = jnp.concatenate([gate_t[...]] * (share // 128), axis=1)
        middle = None
        first = jnp.zeros((1, share), F32)
        second = jnp.zeros((1, share), F32)
        for low, high in zip(out_cuts[:-1], out_cuts[1:]):
            rows = slice(low, high)
            mixed = jnp.dot(
                w_out_t[rows, :], attended[head_cols:, :], preferred_element_type=F32
            )
            embedded = jnp.dot(
                w_embed_t[rows, :], latents[step, :, own_tokens], preferred_element_type=F32
            )
            part = embedded + pos_t[rows, :].astype(F32) + gates[rows, :] * mixed
            hidden[rows, :] = part
            if middle is None:
                middle = jnp.mean(part, axis=0, keepdims=True)
            moved = hidden[rows, :] - middle
            first = first + jnp.sum(moved, axis=0, keepdims=True)
            second = second + jnp.sum(moved * moved, axis=0, keepdims=True)
        first = first * (1.0 / width)
        spread = lax.rsqrt(second * (1.0 / width) - first * first + 1e-06)
        normed = ((hidden[...] - (middle + first)) * spread).astype(BF16)
        speed = jnp.dot(w_final[...], normed, preferred_element_type=F32)
        state[...] = state[...] + pace * speed

        @pl.when(step == 0)
        def _():
            first_velocity[...] = speed

        @pl.when(step < fine_steps - 1)
        def _():
            latents[step + 1, :, own_tokens] = state[...].astype(BF16)
            latent_copy(step + 1).start()

        return carry

    lax.fori_loop(0, fine_steps, fine_step, 0)

    time_before = moment(own_block * fine_steps, step_total)
    time_after = moment((own_block + 1) * fine_steps, step_total)
    keep_start = jnp.where(own_block == 0, 0.0, 1.0)
    share_sum = state[...] / time_after - (keep_start / time_before) * starts[...]
    result = share_sum

    @pl.when(above_total > 0)
    def _():
        pl.semaphore_wait(ready_sem, above_total)

    for axis, (place, peers) in enumerate(ring_axes):
        upward = axis == len(ring_axes) - 1
        sums_out[...] = share_sum.astype(BF16)
        copies = []
        for slot, device in enumerate(peers):
            copy = pltpu.make_async_remote_copy(
                src_ref=sums_out,
                dst_ref=sums_in.at[axis, slot],
                send_sem=scan_send.at[axis, slot],
                recv_sem=scan_recv.at[axis, slot],
                device_id=device,
                device_id_type=MESH,
            )
            copies.append(copy)
            if upward:
                pl.when(place + slot + 1 < RING)(copy.start)
            else:
                copy.start()
        if upward:
            corrected[...] = result
        for slot, copy in enumerate(copies):
            if upward:

                @pl.when(place >= slot + 1)
                def _():
                    copy.wait_recv()
                    corrected[...] += sums_in[axis, slot].astype(F32)

            else:
                copy.wait()
                arrived = sums_in[axis, slot].astype(F32)
                earlier = jnp.where(place >= slot + 1, 1.0, 0.0)
                result = result + earlier * arrived
                share_sum = share_sum + arrived
        if upward:
            for slot, copy in enumerate(copies):
                pl.when(place + slot + 1 < RING)(copy.wait_send)
    corrected[...] = time_after * corrected[...]


def hand_over(corrected, first_velocity, corrected_out, first_velocity_out):
    corrected_out[0] = corrected[...]
    first_velocity_out[0] = first_velocity[...]


def on_device(starts, w_embed, pos_embed, mod_table, mod_index, w_qkv, w_out, text_kv, w_final):
    channels, share = starts.shape[1:]
    image, width = pos_embed.shape
    head_cols = w_out.shape[0]
    text_total = text_kv.shape[1]
    text_rows = -(-text_total // 16) * 16
    key_rows = image + text_rows
    text = text_kv.transpose(1, 0, 2)
    vmem = pl.BlockSpec(memory_space=pltpu.VMEM)
    anywhere = pl.BlockSpec(memory_space=pl.ANY)
    corrected, first_velocity = pl.pallas_call(
        functools.partial(kernel, image + text_total),
        out_shape=[jax.ShapeDtypeStruct((channels, share), F32)] * 2,
        in_specs=[
            vmem,
            anywhere,
            anywhere,
            anywhere,
            pl.BlockSpec(memory_space=pltpu.SMEM),
            anywhere,
            anywhere,
            anywhere,
            anywhere,
        ],
        out_specs=[vmem, vmem],
        scratch_shapes=[
            pltpu.VMEM((channels + EXTRA, width), BF16),
            pltpu.VMEM((width, channels), BF16),
            pltpu.VMEM((channels, 128), F32),
            pltpu.VMEM((image, width), BF16),
            pltpu.VMEM((width, share), BF16),
            pltpu.VMEM((8, image), F32),
            pltpu.VMEM((width, share), F32),
            pltpu.VMEM((3, mod_table.shape[0], width), F32),
            pltpu.VMEM((width, 128), F32),
            pltpu.VMEM((3, width, head_cols), BF16),
            pltpu.VMEM((head_cols, width), BF16),
            pltpu.VMEM((width, 2 * head_cols), BF16),
            pltpu.VMEM((text_total, 2, head_cols), BF16),
            pltpu.VMEM((channels, width), BF16),
            pltpu.VMEM((2, channels, image), BF16),
            pltpu.VMEM((channels, share), F32),
            pltpu.VMEM((image, width), BF16),
            pltpu.VMEM((head_cols, image), BF16),
            pltpu.VMEM((key_rows, head_cols), BF16),
            pltpu.VMEM((head_cols, key_rows), BF16),
            pltpu.VMEM((key_rows, share), F32),
            pltpu.VMEM((key_rows, share), F32),
            pltpu.VMEM((3 * head_cols, share), BF16),
            pltpu.VMEM((channels, share), BF16),
            pltpu.VMEM((3, RING - 1, channels, share), BF16),
            pltpu.SemaphoreType.DMA((21,)),
            pltpu.SemaphoreType.REGULAR,
            pltpu.SemaphoreType.DMA((2,)),
            pltpu.SemaphoreType.DMA((2,)),
            pltpu.SemaphoreType.DMA((2,)),
            pltpu.SemaphoreType.DMA((2,)),
            pltpu.SemaphoreType.DMA,
            pltpu.SemaphoreType.DMA,
            pltpu.SemaphoreType.DMA((3, RING - 1)),
            pltpu.SemaphoreType.DMA((3, RING - 1)),
        ],
        compiler_params=pltpu.CompilerParams(
            collective_id=0, has_side_effects=True, vmem_limit_bytes=63 << 20
        ),
    )(
        starts[0],
        w_embed,
        pos_embed,
        mod_table.transpose(1, 0, 2),
        mod_index,
        w_qkv.transpose(1, 0, 2),
        w_out,
        text,
        w_final.T,
    )
    shape = jax.ShapeDtypeStruct((1, channels, share), F32)
    return pl.pallas_call(
        hand_over,
        out_shape=[shape] * 2,
        in_specs=[vmem, vmem],
        out_specs=[vmem, vmem],
    )(corrected, first_velocity)


def solution(mesh):
    placed = (
        P("tm", None, "seq"),
        P(),
        P(),
        P(),
        P("tm", None),
        P(None, None, "seq"),
        P("seq", None),
        P(None, None, "seq"),
        P(),
    )
    return jax.shard_map(
        on_device,
        mesh=mesh,
        in_specs=placed,
        out_specs=(P("tm", None, "seq"), P("tm", None, "seq")),
        check_vma=False,
    )
```
